512 devices in a mesh: blk: 64 (over x_lo, z, core), group: 8 (over y, x_hi).
Axes of the slice: x: 4 (x_hi: 2, x_lo: 2; x = x_hi * 2 + x_lo), y: 4, z: 16, core: 2. Of those that a mesh axis runs over, the one named last changes fastest.
Arguments:
- queries: bfloat16 [65536, 768], P(('blk', 'group')), may hold values from -6 to 6
- keys: bfloat16 [16384, 768], P(('blk', 'group')), may hold values from -6 to 6
- labels: bfloat16 [16384, 512], P(('blk', 'group')), may hold values from -6 to 6
Outputs:
- soft_labels: bfloat16 [65536, 512], P(('blk', 'group'))
The draws below stay inside these ranges and needn't reach their ends.
All inputs are finite; a program needn't handle non-finite values.
Results may differ from the reference program's by a relative error of at most 0.0035.
Values may be sent and summed in bfloat16 or wider, within the bound.
No kernel may reach another device: no remote copies, remote signals or barrier semaphores. Data moves between devices by JAX's collectives and lax.ppermute only.
A program may use at most 64 MiB of HBM per device.

```python
import math
import jax
import jax.numpy as jnp
from jax import lax

F = 768
C = 512
NQ = 65536
NDB = 16384


def draw_queries(key, part):
    key = jax.random.fold_in(key, 11)
    values = jnp.clip(jax.random.normal(key, (NQ, F), jnp.float32), -6.0, 6.0)
    return values.astype(jnp.bfloat16)


def draw_keys(key, part):
    key = jax.random.fold_in(key, 12)
    values = jnp.clip(jax.random.normal(key, (NDB, F), jnp.float32), -6.0, 6.0)
    return values.astype(jnp.bfloat16)


def level_of(stream_key, extent, cuts, least, high):
    factor_of, own = 1.0, jax.random.fold_in(stream_key, 6)
    for axis_at, blocks in cuts:
        heights = jnp.exp(jax.random.uniform(jax.random.fold_in(own, axis_at), (blocks,), jnp.float32, least / len(cuts), high / len(cuts)))
        factor_of = factor_of * jnp.repeat(heights, extent[axis_at] // blocks).reshape([-1 if axis == axis_at else 1 for axis in range(len(extent))])
    return factor_of


def noise(own_key, dims, width, reach, cuts=(), kind=jnp.bfloat16):
    gain = level_of(own_key, dims, cuts, -0.22, 0.18) if cuts else 1.0
    drawn = jax.random.normal(own_key, dims, jnp.float32) * width * gain
    return jnp.minimum(jnp.maximum(drawn, -reach), reach).astype(kind)


def setup_inputs(seed: int = 0) -> dict:
    seeds = jax.random.split(jax.random.key(seed), 4)
    return {
        "queries": draw_queries(jax.random.fold_in(seeds[3], 71), 0),
        "keys": draw_keys(jax.random.fold_in(seeds[3], 71), 0),
        "labels": noise(seeds[2], (NDB, C), 1.0, 6.0, ((0, 512),)),
    }


def reference(queries, keys, labels):
    sharpness = 2.5 / math.sqrt(F)
    query_blocks = queries.reshape(NQ // 256, 256, F)
    label_values = labels.astype(jnp.float32)

    def classify(query_block):
        scores = jnp.dot(query_block, keys.T, preferred_element_type=jnp.float32) * sharpness
        row_max = lax.optimization_barrier(jnp.max(scores, axis=1, keepdims=True))
        weights = jnp.exp(scores - row_max)
        row_sum = lax.optimization_barrier(jnp.sum(weights, axis=1, keepdims=True))
        weighted = jnp.dot(weights, label_values, preferred_element_type=jnp.float32, precision=lax.Precision.HIGHEST)
        return (weighted / row_sum).astype(jnp.bfloat16)
    return lax.map(classify, query_blocks).reshape(NQ, C)
```

```python
import functools
import math

import jax
import jax.numpy as jnp
from jax import lax
from jax.experimental import pallas as pl
from jax.experimental.pallas import tpu as pltpu
from jax.sharding import Mesh
from jax.sharding import PartitionSpec as P

AXES = ("x_lo", "z_hi", "z_lo", "core", "y", "x_hi")
SIZES = (2, 8, 2, 2, 4, 2)
Z = ("z_hi", "z_lo")
PLANE = ("x_lo", "y", "x_hi")
EXTRA = 16
STEP = 512


def copies(value, count):
    rows, width = value.shape
    return jnp.broadcast_to(value[None], (count, rows, width)).reshape(count * rows, width)


def exchange(value, axes):
    return lax.all_to_all(value, axes, 0, 0, tiled=True)


def shifted(value, axes, by):
    devices = lax.axis_size(axes)
    return lax.ppermute(value, axes, [(i, (i + by) % devices) for i in range(devices)])


def classify(sharpness, *refs):
    *row_refs, queries_ref, out_ref, rows_ref, panel_ref, labels_ref, semaphores = refs
    features = queries_ref.shape[1]
    panels = queries_ref.shape[0] // STEP
    classes, wide = out_ref.shape[1] - EXTRA, out_ref.shape[2]
    fetches, at = [], 0
    for ref in row_refs:
        fetches.append((ref, rows_ref.at[at : at + ref.shape[0], :]))
        at += ref.shape[0]
    for panel in range(panels):
        part = slice(panel * STEP, (panel + 1) * STEP)
        fetches.append((queries_ref.at[part, :], panel_ref.at[part, :]))
    fetches = [
        pltpu.make_async_copy(source, target, semaphores.at[index])
        for index, (source, target) in enumerate(fetches)
    ]
    for fetch in fetches:
        fetch.start()
    for fetch in fetches[: len(row_refs)]:
        fetch.wait()

    def products(panel):
        fetches[len(row_refs) + panel].wait()
        return lax.dot_general(
            rows_ref[:, :features],
            panel_ref[panel * STEP : (panel + 1) * STEP, :],
            (((1,), (1,)), ((), ())),
            preferred_element_type=jnp.float32,
        )

    rate = sharpness * math.log2(math.e)
    row = lax.broadcasted_iota(jnp.int32, (EXTRA, STEP), 0)
    later = products(0)
    labels_ref[...] = rows_ref[:, features:].T
    for panel in range(panels):
        now, later = later, products(panel + 1) if panel + 1 < panels else None
        top = jnp.max(now, axis=0, keepdims=True)
        weights = jnp.exp2((now - top) * rate)
        total = jnp.sum(weights, axis=0, keepdims=True)
        weighted = jnp.dot(
            labels_ref[...], weights.astype(jnp.bfloat16), preferred_element_type=jnp.float32
        )
        mean = (weighted * (1.0 / total)).astype(jnp.bfloat16)
        level = top * sharpness + jnp.log(total)
        first = level.astype(jnp.bfloat16).astype(jnp.float32)
        second = (level - first).astype(jnp.bfloat16).astype(jnp.float32)
        third = level - first - second
        parts = jnp.where(
            row == 0, first, jnp.where(row == 1, second, jnp.where(row == 2, third, 0.0))
        ).astype(jnp.bfloat16)
        for column in range(0, STEP, wide):
            block = (panel * STEP + column) // wide
            out_ref[block, :classes, :] = mean[:, column : column + wide]
            out_ref[block, classes:, :] = parts[:, column : column + wide]


def combine(parts_ref, out_ref):
    sources = parts_ref.shape[0]
    classes = parts_ref.shape[1] - EXTRA
    levels = [
        jnp.sum(parts_ref[source, classes:, :].astype(jnp.float32), axis=0, keepdims=True)
        for source in range(sources)
    ]
    top = functools.reduce(jnp.maximum, levels)
    shares = [jnp.exp(level - top) for level in levels]
    scale = 1.0 / sum(shares)
    shares = [share * scale for share in shares]
    for at in range(0, classes, 128):
        mean = sum(
            shares[source] * parts_ref[source, at : at + 128, :].astype(jnp.float32)
            for source in range(sources)
        )
        out_ref[:, at : at + 128] = mean.T.astype(out_ref.dtype)


def shards(queries, keys, labels):
    count, features = queries.shape
    classes = labels.shape[1]
    plane = lax.axis_size(PLANE)
    sharpness = 2.5 / math.sqrt(features)

    panel = exchange(copies(queries, plane), PLANE)

    rows = jnp.concatenate([keys, labels], axis=1)
    same = lax.all_gather(rows, "z_hi", axis=0, tiled=True)
    half = same.shape[0] // 2
    other = jnp.concatenate([shifted(same[:half], Z, 1), shifted(same[half:], Z, -1)], axis=0)
    row_parts = [same, shifted(same, "core", 1), other, shifted(other, "core", 1)]

    held = sum(part.shape[0] for part in row_parts)
    anywhere = pl.BlockSpec(memory_space=pltpu.HBM)
    parts = pl.pallas_call(
        functools.partial(classify, sharpness),
        in_specs=[anywhere] * (len(row_parts) + 1),
        out_specs=pl.BlockSpec(memory_space=pltpu.VMEM),
        out_shape=jax.ShapeDtypeStruct((plane, classes + EXTRA, count), jnp.bfloat16),
        scratch_shapes=[
            pltpu.VMEM((held, features + classes), jnp.bfloat16),
            pltpu.VMEM((plane * count, features), jnp.bfloat16),
            pltpu.VMEM((classes, held), jnp.bfloat16),
            pltpu.SemaphoreType.DMA((len(row_parts) + plane * count // STEP,)),
        ],
        compiler_params=pltpu.CompilerParams(vmem_limit_bytes=58 * 2**20),
        cost_estimate=pl.CostEstimate(
            flops=2 * plane * count * held * (features + classes),
            bytes_accessed=9 * 2**20,
            transcendentals=plane * count * held,
        ),
        name="classify",
    )(*row_parts, panel)
    parts = exchange(parts, PLANE)
    return pl.pallas_call(
        combine,
        out_shape=jax.ShapeDtypeStruct((count, classes), jnp.bfloat16),
        compiler_params=pltpu.CompilerParams(vmem_limit_bytes=20 * 2**20),
        cost_estimate=pl.CostEstimate(
            flops=2 * plane * count * classes, bytes_accessed=3 * 2**20, transcendentals=0
        ),
        name="combine",
    )(parts)


def solution(mesh):
    chips = Mesh(mesh.devices.reshape(SIZES), AXES)
    placed = P(AXES, None)
    return jax.shard_map(
        shards, mesh=chips, in_specs=(placed, placed, placed), out_specs=placed, check_vma=False
    )
```

```python
import functools
import math

import jax
import jax.numpy as jnp
from jax import lax
from jax.experimental import pallas as pl
from jax.experimental.pallas import tpu as pltpu
from jax.sharding import Mesh
from jax.sharding import PartitionSpec as P

AXES = ("x_lo", "z_hi", "z_lo", "core", "y", "x_hi")
SIZES = (2, 8, 2, 2, 4, 2)
Z = ("z_hi", "z_lo")
PLANE = ("x_lo", "y", "x_hi")
EXTRA = 16
STEP = 512


def copies(value, count):
    rows, width = value.shape
    return jnp.broadcast_to(value[None], (count, rows, width)).reshape(count * rows, width)


def exchange(value, axes):
    return lax.all_to_all(value, axes, 0, 0, tiled=True)


def shifted(value, axes, by):
    devices = lax.axis_size(axes)
    return lax.ppermute(value, axes, [(i, (i + by) % devices) for i in range(devices)])


def classify(sharpness, *refs):
    *row_refs, queries_ref, parts_ref = refs[:-5]
    panel_ref, labels_ref, out_ref, arrivals, departures = refs[-5:]
    features = queries_ref.shape[1]
    panels = queries_ref.shape[0] // STEP
    blocks, classes, wide = out_ref.shape
    classes -= EXTRA
    per_panel = blocks // panels
    held = row_refs[0].shape[0]

    fetches = []
    for panel in range(panels):
        part = slice(panel * STEP, (panel + 1) * STEP)
        fetches.append(
            pltpu.make_async_copy(
                queries_ref.at[part, :], panel_ref.at[part, :], arrivals.at[panel]
            )
        )
    for fetch in fetches:
        fetch.start()
    for index, ref in enumerate(row_refs):
        labels_ref[:, index * held : (index + 1) * held] = ref[:, features:].T

    def products(panel):
        fetches[panel].wait()
        return [
            lax.dot_general(
                ref[:, :features],
                panel_ref[panel * STEP : (panel + 1) * STEP, :],
                (((1,), (1,)), ((), ())),
                preferred_element_type=jnp.float32,
            )
            for ref in row_refs
        ]

    rate = sharpness * math.log2(math.e)
    row = lax.broadcasted_iota(jnp.int32, (EXTRA, STEP), 0)
    later = products(0)
    sends = []
    for panel in range(panels):
        now, later = later, products(panel + 1) if panel + 1 < panels else None
        top = functools.reduce(jnp.maximum, [jnp.max(part, axis=0, keepdims=True) for part in now])
        weights = [jnp.exp2((part - top) * rate) for part in now]
        total = sum(jnp.sum(part, axis=0, keepdims=True) for part in weights)
        weighted = sum(
            jnp.dot(
                labels_ref[:, index * held : (index + 1) * held],
                part.astype(jnp.bfloat16),
                preferred_element_type=jnp.float32,
            )
            for index, part in enumerate(weights)
        )
        mean = (weighted * (1.0 / total)).astype(jnp.bfloat16)
        level = top * sharpness + jnp.log(total)
        first = level.astype(jnp.bfloat16).astype(jnp.float32)
        second = (level - first).astype(jnp.bfloat16).astype(jnp.float32)
        third = level - first - second
        parts = jnp.where(
            row == 0, first, jnp.where(row == 1, second, jnp.where(row == 2, third, 0.0))
        ).astype(jnp.bfloat16)
        for index in range(per_panel):
            block = panel * per_panel + index
            out_ref[block, :classes, :] = mean[:, index * wide : (index + 1) * wide]
            out_ref[block, classes:, :] = parts[:, index * wide : (index + 1) * wide]
        done = slice(panel * per_panel, (panel + 1) * per_panel)
        send = pltpu.make_async_copy(out_ref.at[done], parts_ref.at[done], departures.at[panel])
        send.start()
        sends.append(send)
    for send in sends:
        send.wait()


def combine(parts_ref, out_ref):
    sources = parts_ref.shape[0]
    classes = parts_ref.shape[1] - EXTRA
    levels = [
        jnp.sum(parts_ref[source, classes:, :].astype(jnp.float32), axis=0, keepdims=True)
        for source in range(sources)
    ]
    top = functools.reduce(jnp.maximum, levels)
    shares = [jnp.exp(level - top) for level in levels]
    scale = 1.0 / sum(shares)
    shares = [share * scale for share in shares]
    for at in range(0, classes, 128):
        mean = sum(
            shares[source] * parts_ref[source, at : at + 128, :].astype(jnp.float32)
            for source in range(sources)
        )
        out_ref[:, at : at + 128] = mean.T.astype(out_ref.dtype)


def shards(queries, keys, labels):
    count, features = queries.shape
    classes = labels.shape[1]
    plane = lax.axis_size(PLANE)
    sharpness = 2.5 / math.sqrt(features)

    anywhere = pl.BlockSpec(memory_space=pltpu.HBM)
    inside = pl.BlockSpec(memory_space=pltpu.VMEM)
    panel = exchange(copies(queries, plane), PLANE)

    rows = jnp.concatenate([keys, labels], axis=1)
    same = lax.all_gather(rows, "z_hi", axis=0, tiled=True)
    middle = same.shape[0] // 2
    other = jnp.concatenate([shifted(same[:middle], Z, 1), shifted(same[middle:], Z, -1)], axis=0)
    parts = [same, shifted(same, "core", 1), other, shifted(other, "core", 1)]

    held = sum(part.shape[0] for part in parts)
    blocks = (plane, classes + EXTRA, count)
    parts = pl.pallas_call(
        functools.partial(classify, sharpness),
        in_specs=[inside] * len(parts) + [anywhere],
        out_specs=anywhere,
        out_shape=jax.ShapeDtypeStruct(blocks, jnp.bfloat16),
        scratch_shapes=[
            pltpu.VMEM((plane * count, features), jnp.bfloat16),
            pltpu.VMEM((classes, held), jnp.bfloat16),
            pltpu.VMEM(blocks, jnp.bfloat16),
            pltpu.SemaphoreType.DMA((plane * count // STEP,)),
            pltpu.SemaphoreType.DMA((plane * count // STEP,)),
        ],
        compiler_params=pltpu.CompilerParams(vmem_limit_bytes=48 * 2**20),
        cost_estimate=pl.CostEstimate(
            flops=2 * plane * count * held * (features + classes),
            bytes_accessed=9 * 2**20,
            transcendentals=plane * count * held,
        ),
        name="classify",
    )(*parts, panel)
    parts = exchange(parts, PLANE)
    return pl.pallas_call(
        combine,
        out_shape=jax.ShapeDtypeStruct((count, classes), jnp.bfloat16),
        compiler_params=pltpu.CompilerParams(vmem_limit_bytes=20 * 2**20),
        cost_estimate=pl.CostEstimate(
            flops=2 * plane * count * classes, bytes_accessed=3 * 2**20, transcendentals=0
        ),
        name="combine",
    )(parts)


def solution(mesh):
    chips = Mesh(mesh.devices.reshape(SIZES), AXES)
    placed = P(AXES, None)
    return jax.shard_map(
        shards, mesh=chips, in_specs=(placed, placed, placed), out_specs=placed, check_vma=False
    )
```

```python
import functools
import math

import jax
import jax.numpy as jnp
from jax import lax
from jax.experimental import pallas as pl
from jax.experimental.pallas import tpu as pltpu
from jax.sharding import Mesh
from jax.sharding import PartitionSpec as P

AXES = ("x_lo", "z_hi", "z_lo", "core", "y", "x_hi")
SIZES = (2, 8, 2, 2, 4, 2)
ZX = ("x_lo", "z_hi", "z_lo", "x_hi")
GROUP = ("y", "x_hi")
EXTRA = 16
STEP = 512


def copies(value, count):
    rows, width = value.shape
    return jnp.broadcast_to(value[None], (count, rows, width)).reshape(count * rows, width)


def exchange(value, axes):
    return lax.all_to_all(value, axes, 0, 0, tiled=True)


def moved(value, along_x, along_z):
    columns = lax.axis_size("x_lo") * lax.axis_size("x_hi")
    height = lax.axis_size("z_hi") * lax.axis_size("z_lo")

    def place(x, z):
        x, z = x % columns, z % height
        return ((x % 2) * height + z) * 2 + x // 2

    return lax.ppermute(
        value,
        ZX,
        [
            (place(x, z), place(x + along_x, z + along_z))
            for x in range(columns)
            for z in range(height)
        ],
    )


def swapped(value):
    return lax.ppermute(value, "core", [(0, 1), (1, 0)])


def classify(sharpness, pieces, resumes, ends, *refs):
    refs = list(refs)
    row_refs, refs = refs[:pieces], refs[pieces:]
    queries_ref = refs.pop(0)
    if resumes:
        past_ref, past_stats_ref = refs.pop(0), refs.pop(0)
    if ends:
        parts_ref, labels_ref, out_ref, departures = refs
    else:
        weighted_ref, stats_ref, labels_ref = refs
    features = queries_ref.shape[1]
    panels = queries_ref.shape[0] // STEP
    bounds = [0]
    for ref in row_refs:
        bounds.append(bounds[-1] + ref.shape[0])
    for index, ref in enumerate(row_refs):
        labels_ref[:, bounds[index] : bounds[index + 1]] = ref[:, features:].T

    def products(panel):
        return [
            lax.dot_general(
                ref[:, :features],
                queries_ref[panel * STEP : (panel + 1) * STEP, :],
                (((1,), (1,)), ((), ())),
                preferred_element_type=jnp.float32,
            )
            for ref in row_refs
        ]

    rate = sharpness * math.log2(math.e)
    later = products(0)
    sends = []
    for panel in range(panels):
        now, later = later, products(panel + 1) if panel + 1 < panels else None
        columns = slice(panel * STEP, (panel + 1) * STEP)
        top = functools.reduce(jnp.maximum, [jnp.max(part, axis=0, keepdims=True) for part in now])
        if resumes:
            past_top = past_stats_ref[0:1, columns]
            top = jnp.maximum(top, past_top)
            fade = jnp.exp2((past_top - top) * rate)
        weights = [jnp.exp2((part - top) * rate) for part in now]
        total = sum(jnp.sum(part, axis=0, keepdims=True) for part in weights)
        weighted = sum(
            jnp.dot(
                labels_ref[:, bounds[index] : bounds[index + 1]],
                part.astype(jnp.bfloat16),
                preferred_element_type=jnp.float32,
            )
            for index, part in enumerate(weights)
        )
        if resumes:
            total = total + fade * past_stats_ref[1:2, columns]
            weighted = weighted + fade * past_ref[:, columns]
        if not ends:
            weighted_ref[:, columns] = weighted
            stats_ref[0:1, columns] = top
            stats_ref[1:2, columns] = total
            continue
        mean = (weighted * (1.0 / total)).astype(jnp.bfloat16)
        level = top * sharpness + jnp.log(total)
        first = level.astype(jnp.bfloat16).astype(jnp.float32)
        second = (level - first).astype(jnp.bfloat16).astype(jnp.float32)
        third = level - first - second
        row = lax.broadcasted_iota(jnp.int32, (EXTRA, STEP), 0)
        levels = jnp.where(
            row == 0, first, jnp.where(row == 1, second, jnp.where(row == 2, third, 0.0))
        ).astype(jnp.bfloat16)
        blocks, classes, wide = out_ref.shape
        classes -= EXTRA
        per_panel = blocks // panels
        for index in range(per_panel):
            block = panel * per_panel + index
            out_ref[block, :classes, :] = mean[:, index * wide : (index + 1) * wide]
            out_ref[block, classes:, :] = levels[:, index * wide : (index + 1) * wide]
        done = slice(panel * per_panel, (panel + 1) * per_panel)
        send = pltpu.make_async_copy(out_ref.at[done], parts_ref.at[done], departures.at[panel])
        send.start()
        sends.append(send)
    for send in sends:
        send.wait()


def combine(parts_ref, out_ref):
    sources = parts_ref.shape[0]
    classes = parts_ref.shape[1] - EXTRA
    levels = [
        jnp.sum(parts_ref[source, classes:, :].astype(jnp.float32), axis=0, keepdims=True)
        for source in range(sources)
    ]
    top = functools.reduce(jnp.maximum, levels)
    shares = [jnp.exp(level - top) for level in levels]
    scale = 1.0 / sum(shares)
    shares = [share * scale for share in shares]
    for at in range(0, classes, 128):
        mean = sum(
            shares[source] * parts_ref[source, at : at + 128, :].astype(jnp.float32)
            for source in range(sources)
        )
        out_ref[:, at : at + 128] = mean.T.astype(out_ref.dtype)


def shards(queries, keys, labels):
    count, features = queries.shape
    classes = labels.shape[1]
    group = lax.axis_size(GROUP)
    anywhere = pl.BlockSpec(memory_space=pltpu.HBM)
    inside = pl.BlockSpec(memory_space=pltpu.VMEM)
    sharpness = 2.5 / math.sqrt(features)

    panel = exchange(copies(queries, group), GROUP)

    rows = jnp.concatenate([keys, labels], axis=1)
    same = lax.all_gather(rows, "z_hi", axis=0, tiled=True)
    same, panel = lax.optimization_barrier((same, panel))
    others = [moved(same, 1, -1), moved(same, 0, 1), moved(same, -1, 0)]

    blocks = (group, classes + EXTRA, count)
    asked = group * count

    def taken(row_parts, running, ends):
        held = sum(part.shape[0] for part in row_parts)
        operands = [*row_parts, panel, *running]
        scratch = [pltpu.VMEM((classes, held), jnp.bfloat16)]
        if ends:
            out_specs = anywhere
            out_shape = jax.ShapeDtypeStruct(blocks, jnp.bfloat16)
            scratch += [
                pltpu.VMEM(blocks, jnp.bfloat16),
                pltpu.SemaphoreType.DMA((asked // STEP,)),
            ]
        else:
            out_specs = [inside, inside]
            out_shape = [
                jax.ShapeDtypeStruct((classes, asked), jnp.float32),
                jax.ShapeDtypeStruct((8, asked), jnp.float32),
            ]
        return pl.pallas_call(
            functools.partial(classify, sharpness, len(row_parts), bool(running), ends),
            in_specs=[inside] * len(operands),
            out_specs=out_specs,
            out_shape=out_shape,
            scratch_shapes=scratch,
            compiler_params=pltpu.CompilerParams(vmem_limit_bytes=40 * 2**20),
            cost_estimate=pl.CostEstimate(
                flops=2 * asked * held * (features + classes),
                bytes_accessed=4 * 2**20,
                transcendentals=asked * held,
            ),
            name="classify",
        )(*operands)

    others = jnp.concatenate(others, axis=0)
    near = jnp.concatenate([same, others], axis=0)
    running = taken([near], (), False)
    parts = taken([swapped(near)], running, True)
    parts = exchange(parts, GROUP)
    return pl.pallas_call(
        combine,
        out_shape=jax.ShapeDtypeStruct((count, classes), jnp.bfloat16),
        compiler_params=pltpu.CompilerParams(vmem_limit_bytes=20 * 2**20),
        cost_estimate=pl.CostEstimate(
            flops=2 * group * count * classes, bytes_accessed=3 * 2**20, transcendentals=0
        ),
        name="combine",
    )(parts)


def solution(mesh):
    chips = Mesh(mesh.devices.reshape(SIZES), AXES)
    placed = P(AXES, None)
    return jax.shard_map(
        shards, mesh=chips, in_specs=(placed, placed, placed), out_specs=placed, check_vma=False
    )
```

```python
import functools
import math

import jax
import jax.numpy as jnp
from jax import lax
from jax.experimental import pallas as pl
from jax.experimental.pallas import tpu as pltpu
from jax.sharding import Mesh
from jax.sharding import PartitionSpec as P

AXES = ("x_lo", "z_hi", "z_lo", "core", "y", "x_hi")
SIZES = (2, 8, 2, 2, 4, 2)
ZX = ("x_lo", "z_hi", "z_lo", "x_hi")
GROUP = ("y", "x_hi")
EXTRA = 16
STEP = 512


def copies(value, count):
    rows, width = value.shape
    return jnp.broadcast_to(value[None], (count, rows, width)).reshape(count * rows, width)


def exchange(value, axes):
    return lax.all_to_all(value, axes, 0, 0, tiled=True)


def moved(value, along_x, along_z):
    columns = lax.axis_size("x_lo") * lax.axis_size("x_hi")
    height = lax.axis_size("z_hi") * lax.axis_size("z_lo")

    def place(x, z):
        x, z = x % columns, z % height
        return ((x % 2) * height + z) * 2 + x // 2

    return lax.ppermute(
        value,
        ZX,
        [
            (place(x, z), place(x + along_x, z + along_z))
            for x in range(columns)
            for z in range(height)
        ],
    )


def swapped(value):
    return lax.ppermute(value, "core", [(0, 1), (1, 0)])


def classify(sharpness, pieces, resumes, ends, *refs):
    refs = list(refs)
    row_refs, refs = refs[:pieces], refs[pieces:]
    queries_ref = refs.pop(0)
    if resumes:
        past_ref, past_stats_ref = refs.pop(0), refs.pop(0)
    if ends:
        out_ref, labels_ref = refs
    else:
        weighted_ref, stats_ref, labels_ref = refs
    features = queries_ref.shape[1]
    panels = queries_ref.shape[0] // STEP
    bounds = [0]
    for ref in row_refs:
        bounds.append(bounds[-1] + ref.shape[0])
    for index, ref in enumerate(row_refs):
        labels_ref[:, bounds[index] : bounds[index + 1]] = ref[:, features:].T

    def products(panel):
        return [
            lax.dot_general(
                ref[:, :features],
                queries_ref[panel * STEP : (panel + 1) * STEP, :],
                (((1,), (1,)), ((), ())),
                preferred_element_type=jnp.float32,
            )
            for ref in row_refs
        ]

    rate = sharpness * math.log2(math.e)
    later = products(0)
    for panel in range(panels):
        now, later = later, products(panel + 1) if panel + 1 < panels else None
        columns = slice(panel * STEP, (panel + 1) * STEP)
        top = functools.reduce(jnp.maximum, [jnp.max(part, axis=0, keepdims=True) for part in now])
        if resumes:
            past_top = past_stats_ref[0:1, columns]
            top = jnp.maximum(top, past_top)
            fade = jnp.exp2((past_top - top) * rate)
        weights = [jnp.exp2((part - top) * rate) for part in now]
        total = sum(jnp.sum(part, axis=0, keepdims=True) for part in weights)
        weighted = sum(
            jnp.dot(
                labels_ref[:, bounds[index] : bounds[index + 1]],
                part.astype(jnp.bfloat16),
                preferred_element_type=jnp.float32,
            )
            for index, part in enumerate(weights)
        )
        if resumes:
            total = total + fade * past_stats_ref[1:2, columns]
            weighted = weighted + fade * past_ref[:, columns]
        if not ends:
            weighted_ref[:, columns] = weighted
            stats_ref[0:1, columns] = top
            stats_ref[1:2, columns] = total
            continue
        mean = (weighted * (1.0 / total)).astype(jnp.bfloat16)
        level = top * sharpness + jnp.log(total)
        first = level.astype(jnp.bfloat16).astype(jnp.float32)
        second = (level - first).astype(jnp.bfloat16).astype(jnp.float32)
        third = level - first - second
        row = lax.broadcasted_iota(jnp.int32, (EXTRA, STEP), 0)
        levels = jnp.where(
            row == 0, first, jnp.where(row == 1, second, jnp.where(row == 2, third, 0.0))
        ).astype(jnp.bfloat16)
        blocks, classes, wide = out_ref.shape
        classes -= EXTRA
        per_panel = blocks // panels
        for index in range(per_panel):
            block = panel * per_panel + index
            out_ref[block, :classes, :] = mean[:, index * wide : (index + 1) * wide]
            out_ref[block, classes:, :] = levels[:, index * wide : (index + 1) * wide]


def combine(parts_ref, out_ref):
    sources = parts_ref.shape[0]
    classes = parts_ref.shape[1] - EXTRA
    levels = [
        jnp.sum(parts_ref[source, classes:, :].astype(jnp.float32), axis=0, keepdims=True)
        for source in range(sources)
    ]
    top = functools.reduce(jnp.maximum, levels)
    shares = [jnp.exp(level - top) for level in levels]
    scale = 1.0 / sum(shares)
    shares = [share * scale for share in shares]
    for at in range(0, classes, 128):
        mean = sum(
            shares[source] * parts_ref[source, at : at + 128, :].astype(jnp.float32)
            for source in range(sources)
        )
        out_ref[:, at : at + 128] = mean.T.astype(out_ref.dtype)


def shards(queries, keys, labels):
    count, features = queries.shape
    classes = labels.shape[1]
    group = lax.axis_size(GROUP)
    inside = pl.BlockSpec(memory_space=pltpu.VMEM)
    sharpness = 2.5 / math.sqrt(features)

    panel = exchange(copies(queries, group), GROUP)

    rows = jnp.concatenate([keys, labels], axis=1)
    same = lax.all_gather(rows, "z_hi", axis=0, tiled=True)
    same, panel = lax.optimization_barrier((same, panel))
    others = [moved(same, -1, 0), moved(same, 0, 1), moved(same, 1, -1)]

    blocks = (group, classes + EXTRA, count)
    asked = group * count

    def taken(row_parts, running, ends):
        held = sum(part.shape[0] for part in row_parts)
        operands = [*row_parts, panel, *running]
        scratch = [pltpu.VMEM((classes, held), jnp.bfloat16)]
        if ends:
            out_specs = inside
            out_shape = jax.ShapeDtypeStruct(blocks, jnp.bfloat16)
        else:
            out_specs = [inside, inside]
            out_shape = [
                jax.ShapeDtypeStruct((classes, asked), jnp.float32),
                jax.ShapeDtypeStruct((8, asked), jnp.float32),
            ]
        return pl.pallas_call(
            functools.partial(classify, sharpness, len(row_parts), bool(running), ends),
            in_specs=[inside] * len(operands),
            out_specs=out_specs,
            out_shape=out_shape,
            scratch_shapes=scratch,
            compiler_params=pltpu.CompilerParams(vmem_limit_bytes=40 * 2**20),
            cost_estimate=pl.CostEstimate(
                flops=2 * asked * held * (features + classes),
                bytes_accessed=4 * 2**20,
                transcendentals=asked * held,
            ),
            name="classify",
        )(*operands)

    running = taken([same], (), False)
    same_late, running = lax.optimization_barrier((same, running))
    far_same = swapped(same_late)
    others, far_same = lax.optimization_barrier((others, far_same))
    others = jnp.concatenate(others, axis=0)
    running = taken([others, far_same], running, False)
    parts = taken([swapped(others)], running, True)
    parts = exchange(parts, GROUP)
    return pl.pallas_call(
        combine,
        out_shape=jax.ShapeDtypeStruct((count, classes), jnp.bfloat16),
        compiler_params=pltpu.CompilerParams(vmem_limit_bytes=20 * 2**20),
        cost_estimate=pl.CostEstimate(
            flops=2 * group * count * classes, bytes_accessed=3 * 2**20, transcendentals=0
        ),
        name="combine",
    )(parts)


def solution(mesh):
    chips = Mesh(mesh.devices.reshape(SIZES), AXES)
    placed = P(AXES, None)
    return jax.shard_map(
        shards, mesh=chips, in_specs=(placed, placed, placed), out_specs=placed, check_vma=False
    )
```

```python
import functools
import math

import jax
import jax.numpy as jnp
from jax import lax
from jax.experimental import pallas as pl
from jax.experimental.pallas import tpu as pltpu
from jax.sharding import Mesh
from jax.sharding import PartitionSpec as P

AXES = ("x_lo", "z_hi", "z_lo", "core", "y", "x_hi")
SIZES = (2, 8, 2, 2, 4, 2)
ZX = ("x_lo", "z_hi", "z_lo", "x_hi")
GROUP = ("y", "x_hi")
EXTRA = 16
STEP = 512


def copies(value, count):
    rows, width = value.shape
    return jnp.broadcast_to(value[None], (count, rows, width)).reshape(count * rows, width)


def exchange(value, axes):
    return lax.all_to_all(value, axes, 0, 0, tiled=True)


def moved(value, along_x, along_z):
    columns = lax.axis_size("x_lo") * lax.axis_size("x_hi")
    height = lax.axis_size("z_hi") * lax.axis_size("z_lo")

    def place(x, z):
        x, z = x % columns, z % height
        return ((x % 2) * height + z) * 2 + x // 2

    return lax.ppermute(
        value,
        ZX,
        [
            (place(x, z), place(x + along_x, z + along_z))
            for x in range(columns)
            for z in range(height)
        ],
    )


def swapped(value):
    return lax.ppermute(value, "core", [(0, 1), (1, 0)])


def classify(sharpness, pieces, resumes, ends, *refs):
    refs = list(refs)
    row_refs, refs = refs[:pieces], refs[pieces:]
    queries_ref = refs.pop(0)
    if resumes:
        past_ref, past_stats_ref = refs.pop(0), refs.pop(0)
    if ends:
        out_ref, labels_ref = refs
    else:
        weighted_ref, stats_ref, labels_ref = refs
    features = queries_ref.shape[1]
    panels = queries_ref.shape[0] // STEP
    bounds = [0]
    for ref in row_refs:
        bounds.append(bounds[-1] + ref.shape[0])
    for index, ref in enumerate(row_refs):
        labels_ref[:, bounds[index] : bounds[index + 1]] = ref[:, features:].T

    def products(panel):
        return [
            lax.dot_general(
                ref[:, :features],
                queries_ref[panel * STEP : (panel + 1) * STEP, :],
                (((1,), (1,)), ((), ())),
                preferred_element_type=jnp.float32,
            )
            for ref in row_refs
        ]

    rate = sharpness * math.log2(math.e)
    later = products(0)
    for panel in range(panels):
        now, later = later, products(panel + 1) if panel + 1 < panels else None
        columns = slice(panel * STEP, (panel + 1) * STEP)
        top = functools.reduce(jnp.maximum, [jnp.max(part, axis=0, keepdims=True) for part in now])
        if resumes:
            past_top = past_stats_ref[0:1, columns]
            top = jnp.maximum(top, past_top)
            fade = jnp.exp2((past_top - top) * rate)
        weights = [jnp.exp2((part - top) * rate).astype(jnp.bfloat16) for part in now]
        total = sum(
            jnp.sum(part.astype(jnp.float32), axis=0, keepdims=True) for part in weights
        )
        weighted = sum(
            jnp.dot(
                labels_ref[:, bounds[index] : bounds[index + 1]],
                part,
                preferred_element_type=jnp.float32,
            )
            for index, part in enumerate(weights)
        )
        if resumes:
            total = total + fade * past_stats_ref[1:2, columns]
            weighted = weighted + fade * past_ref[:, columns]
        if not ends:
            weighted_ref[:, columns] = weighted
            stats_ref[0:1, columns] = top
            stats_ref[1:2, columns] = total
            continue
        mean = (weighted * (1.0 / total)).astype(jnp.bfloat16)
        level = top * sharpness + jnp.log(total)
        first = level.astype(jnp.bfloat16).astype(jnp.float32)
        second = (level - first).astype(jnp.bfloat16).astype(jnp.float32)
        third = level - first - second
        row = lax.broadcasted_iota(jnp.int32, (EXTRA, STEP), 0)
        levels = jnp.where(
            row == 0, first, jnp.where(row == 1, second, jnp.where(row == 2, third, 0.0))
        ).astype(jnp.bfloat16)
        blocks, classes, wide = out_ref.shape
        classes -= EXTRA
        per_panel = blocks // panels
        for index in range(per_panel):
            block = panel * per_panel + index
            out_ref[block, :classes, :] = mean[:, index * wide : (index + 1) * wide]
            out_ref[block, classes:, :] = levels[:, index * wide : (index + 1) * wide]


def combine(parts_ref, out_ref):
    sources = parts_ref.shape[0]
    classes = parts_ref.shape[1] - EXTRA
    levels = [
        jnp.sum(parts_ref[source, classes:, :].astype(jnp.float32), axis=0, keepdims=True)
        for source in range(sources)
    ]
    top = functools.reduce(jnp.maximum, levels)
    shares = [jnp.exp(level - top) for level in levels]
    scale = 1.0 / sum(shares)
    shares = [share * scale for share in shares]
    for at in range(0, classes, 128):
        mean = sum(
            shares[source] * parts_ref[source, at : at + 128, :].astype(jnp.float32)
            for source in range(sources)
        )
        out_ref[:, at : at + 128] = mean.T.astype(out_ref.dtype)


def shards(queries, keys, labels):
    count, features = queries.shape
    classes = labels.shape[1]
    group = lax.axis_size(GROUP)
    inside = pl.BlockSpec(memory_space=pltpu.VMEM)
    sharpness = 2.5 / math.sqrt(features)

    panel = exchange(copies(queries, group), GROUP)

    rows = jnp.concatenate([keys, labels], axis=1)
    same = lax.all_gather(rows, "z_hi", axis=0, tiled=True)
    same, panel = lax.optimization_barrier((same, panel))
    others = [moved(same, -1, 0), moved(same, 0, 1), moved(same, 1, -1)]

    blocks = (group, classes + EXTRA, count)
    asked = group * count

    def taken(row_parts, running, ends):
        held = sum(part.shape[0] for part in row_parts)
        operands = [*row_parts, panel, *running]
        scratch = [pltpu.VMEM((classes, held), jnp.bfloat16)]
        if ends:
            out_specs = inside
            out_shape = jax.ShapeDtypeStruct(blocks, jnp.bfloat16)
        else:
            out_specs = [inside, inside]
            out_shape = [
                jax.ShapeDtypeStruct((classes, asked), jnp.float32),
                jax.ShapeDtypeStruct((8, asked), jnp.float32),
            ]
        return pl.pallas_call(
            functools.partial(classify, sharpness, len(row_parts), bool(running), ends),
            in_specs=[inside] * len(operands),
            out_specs=out_specs,
            out_shape=out_shape,
            scratch_shapes=scratch,
            compiler_params=pltpu.CompilerParams(vmem_limit_bytes=40 * 2**20),
            cost_estimate=pl.CostEstimate(
                flops=2 * asked * held * (features + classes),
                bytes_accessed=4 * 2**20,
                transcendentals=asked * held,
            ),
            name="classify",
        )(*operands)

    running = taken([same], (), False)
    same_late, running = lax.optimization_barrier((same, running))
    far_same = swapped(same_late)
    others, far_same = lax.optimization_barrier((others, far_same))
    others = jnp.concatenate(others, axis=0)
    running = taken([others, far_same], running, False)
    parts = taken([swapped(others)], running, True)
    parts = exchange(parts, GROUP)
    return pl.pallas_call(
        combine,
        out_shape=jax.ShapeDtypeStruct((count, classes), jnp.bfloat16),
        compiler_params=pltpu.CompilerParams(vmem_limit_bytes=20 * 2**20),
        cost_estimate=pl.CostEstimate(
            flops=2 * group * count * classes, bytes_accessed=3 * 2**20, transcendentals=0
        ),
        name="combine",
    )(parts)


def solution(mesh):
    chips = Mesh(mesh.devices.reshape(SIZES), AXES)
    placed = P(AXES, None)
    return jax.shard_map(
        shards, mesh=chips, in_specs=(placed, placed, placed), out_specs=placed, check_vma=False
    )
```

```python
import functools
import math

import jax
import jax.numpy as jnp
from jax import lax
from jax.experimental import pallas as pl
from jax.experimental.pallas import tpu as pltpu
from jax.sharding import Mesh
from jax.sharding import PartitionSpec as P

AXES = ("x_lo", "z_hi", "z_lo", "core", "y", "x_hi")
SIZES = (2, 8, 2, 2, 4, 2)
ZX = ("x_lo", "z_hi", "z_lo", "core", "x_hi")
GROUP = ("y", "x_hi")
EXTRA = 16
STEP = 512


def copies(value, count):
    rows, width = value.shape
    return jnp.broadcast_to(value[None], (count, rows, width)).reshape(count * rows, width)


def exchange(value, axes):
    return lax.all_to_all(value, axes, 0, 0, tiled=True)


def moved(value, along_x, along_z):
    columns = lax.axis_size("x_lo") * lax.axis_size("x_hi")
    height = lax.axis_size("z_hi") * lax.axis_size("z_lo")

    def place(x, z, core):
        x, z = x % columns, z % height
        return (((x % 2) * height + z) * 2 + core) * 2 + x // 2

    return lax.ppermute(
        value,
        ZX,
        [
            (place(x, z, core), place(x + sign * along_x, z + sign * along_z, core))
            for core, sign in ((0, 1), (1, -1))
            for x in range(columns)
            for z in range(height)
        ],
    )


def swapped(value):
    return lax.ppermute(value, "core", [(0, 1), (1, 0)])


def classify(sharpness, pieces, resumes, ends, *refs):
    refs = list(refs)
    row_refs, refs = refs[:pieces], refs[pieces:]
    queries_ref = refs.pop(0)
    if resumes:
        past_ref, past_stats_ref = refs.pop(0), refs.pop(0)
    if ends:
        out_ref, labels_ref = refs
    else:
        weighted_ref, stats_ref, labels_ref = refs
    features = queries_ref.shape[1]
    panels = queries_ref.shape[0] // STEP
    bounds = [0]
    for ref in row_refs:
        bounds.append(bounds[-1] + ref.shape[0])
    for index, ref in enumerate(row_refs):
        labels_ref[:, bounds[index] : bounds[index + 1]] = ref[:, features:].T

    def products(panel):
        return [
            lax.dot_general(
                ref[:, :features],
                queries_ref[panel * STEP : (panel + 1) * STEP, :],
                (((1,), (1,)), ((), ())),
                preferred_element_type=jnp.float32,
            )
            for ref in row_refs
        ]

    rate = sharpness * math.log2(math.e)
    later = products(0)
    for panel in range(panels):
        now, later = later, products(panel + 1) if panel + 1 < panels else None
        columns = slice(panel * STEP, (panel + 1) * STEP)
        top = functools.reduce(jnp.maximum, [jnp.max(part, axis=0, keepdims=True) for part in now])
        if resumes:
            past_top = past_stats_ref[0:1, columns]
            top = jnp.maximum(top, past_top)
            fade = jnp.exp2((past_top - top) * rate)
        weights = [jnp.exp2((part - top) * rate).astype(jnp.bfloat16) for part in now]
        total = sum(
            jnp.sum(part.astype(jnp.float32), axis=0, keepdims=True) for part in weights
        )
        weighted = sum(
            jnp.dot(
                labels_ref[:, bounds[index] : bounds[index + 1]],
                part,
                preferred_element_type=jnp.float32,
            )
            for index, part in enumerate(weights)
        )
        if resumes:
            total = total + fade * past_stats_ref[1:2, columns]
            weighted = weighted + fade * past_ref[:, columns]
        if not ends:
            weighted_ref[:, columns] = weighted
            stats_ref[0:1, columns] = top
            stats_ref[1:2, columns] = total
            continue
        mean = (weighted * (1.0 / total)).astype(jnp.bfloat16)
        level = top * sharpness + jnp.log(total)
        first = level.astype(jnp.bfloat16).astype(jnp.float32)
        second = (level - first).astype(jnp.bfloat16).astype(jnp.float32)
        third = level - first - second
        row = lax.broadcasted_iota(jnp.int32, (EXTRA, STEP), 0)
        levels = jnp.where(
            row == 0, first, jnp.where(row == 1, second, jnp.where(row == 2, third, 0.0))
        ).astype(jnp.bfloat16)
        blocks, classes, wide = out_ref.shape
        classes -= EXTRA
        per_panel = blocks // panels
        for index in range(per_panel):
            block = panel * per_panel + index
            out_ref[block, :classes, :] = mean[:, index * wide : (index + 1) * wide]
            out_ref[block, classes:, :] = levels[:, index * wide : (index + 1) * wide]


def combine(parts_ref, out_ref):
    sources = parts_ref.shape[0]
    classes = parts_ref.shape[1] - EXTRA
    levels = [
        jnp.sum(parts_ref[source, classes:, :].astype(jnp.float32), axis=0, keepdims=True)
        for source in range(sources)
    ]
    top = functools.reduce(jnp.maximum, levels)
    shares = [jnp.exp(level - top) for level in levels]
    scale = 1.0 / sum(shares)
    shares = [share * scale for share in shares]
    for at in range(0, classes, 128):
        mean = sum(
            shares[source] * parts_ref[source, at : at + 128, :].astype(jnp.float32)
            for source in range(sources)
        )
        out_ref[:, at : at + 128] = mean.T.astype(out_ref.dtype)


def shards(queries, keys, labels):
    count, features = queries.shape
    classes = labels.shape[1]
    group = lax.axis_size(GROUP)
    inside = pl.BlockSpec(memory_space=pltpu.VMEM)
    sharpness = 2.5 / math.sqrt(features)

    panel = exchange(copies(queries, group), GROUP)

    rows = jnp.concatenate([keys, labels], axis=1)
    same = lax.all_gather(rows, "z_hi", axis=0, tiled=True)
    same, panel = lax.optimization_barrier((same, panel))
    others = [moved(same, -1, 0), moved(same, 0, 1), moved(same, 1, -1)]

    blocks = (group, classes + EXTRA, count)
    asked = group * count

    def taken(row_parts, running, ends):
        held = sum(part.shape[0] for part in row_parts)
        operands = [*row_parts, panel, *running]
        scratch = [pltpu.VMEM((classes, held), jnp.bfloat16)]
        if ends:
            out_specs = inside
            out_shape = jax.ShapeDtypeStruct(blocks, jnp.bfloat16)
        else:
            out_specs = [inside, inside]
            out_shape = [
                jax.ShapeDtypeStruct((classes, asked), jnp.float32),
                jax.ShapeDtypeStruct((8, asked), jnp.float32),
            ]
        return pl.pallas_call(
            functools.partial(classify, sharpness, len(row_parts), bool(running), ends),
            in_specs=[inside] * len(operands),
            out_specs=out_specs,
            out_shape=out_shape,
            scratch_shapes=scratch,
            compiler_params=pltpu.CompilerParams(vmem_limit_bytes=40 * 2**20),
            cost_estimate=pl.CostEstimate(
                flops=2 * asked * held * (features + classes),
                bytes_accessed=4 * 2**20,
                transcendentals=asked * held,
            ),
            name="classify",
        )(*operands)

    running = taken([same], (), False)
    same_late, running = lax.optimization_barrier((same, running))
    far_same = swapped(same_late)
    others, far_same = lax.optimization_barrier((others, far_same))
    others = jnp.concatenate(others, axis=0)
    running = taken([others, far_same], running, False)
    parts = taken([swapped(others)], running, True)
    parts = exchange(parts, GROUP)
    return pl.pallas_call(
        combine,
        out_shape=jax.ShapeDtypeStruct((count, classes), jnp.bfloat16),
        compiler_params=pltpu.CompilerParams(vmem_limit_bytes=20 * 2**20),
        cost_estimate=pl.CostEstimate(
            flops=2 * group * count * classes, bytes_accessed=3 * 2**20, transcendentals=0
        ),
        name="combine",
    )(parts)


def solution(mesh):
    chips = Mesh(mesh.devices.reshape(SIZES), AXES)
    placed = P(AXES, None)
    return jax.shard_map(
        shards, mesh=chips, in_specs=(placed, placed, placed), out_specs=placed, check_vma=False
    )
```

```python
import functools
import math

import jax
import jax.numpy as jnp
from jax import lax
from jax.experimental import pallas as pl
from jax.experimental.pallas import tpu as pltpu
from jax.sharding import Mesh
from jax.sharding import PartitionSpec as P

AXES = ("x_lo", "z_hi", "z_lo", "core", "y", "x_hi")
SIZES = (2, 8, 2, 2, 4, 2)
ZX = ("x_lo", "z_hi", "z_lo", "x_hi")
GROUP = ("y", "x_hi")
EXTRA = 16
STEP = 1024


def copies(value, count):
    rows, width = value.shape
    return jnp.broadcast_to(value[None], (count, rows, width)).reshape(count * rows, width)


def exchange(value, axes):
    return lax.all_to_all(value, axes, 0, 0, tiled=True)


def moved(value, along_x, along_z):
    columns = lax.axis_size("x_lo") * lax.axis_size("x_hi")
    height = lax.axis_size("z_hi") * lax.axis_size("z_lo")

    def place(x, z):
        x, z = x % columns, z % height
        return ((x % 2) * height + z) * 2 + x // 2

    return lax.ppermute(
        value,
        ZX,
        [
            (place(x, z), place(x + along_x, z + along_z))
            for x in range(columns)
            for z in range(height)
        ],
    )


def swapped(value):
    return lax.ppermute(value, "core", [(0, 1), (1, 0)])


def classify(sharpness, pieces, resumes, ends, *refs):
    refs = list(refs)
    row_refs, refs = refs[:pieces], refs[pieces:]
    queries_ref = refs.pop(0)
    if resumes:
        past_ref, past_stats_ref = refs.pop(0), refs.pop(0)
    if ends:
        out_ref, labels_ref = refs
    else:
        weighted_ref, stats_ref, labels_ref = refs
    features = queries_ref.shape[1]
    panels = queries_ref.shape[0] // STEP
    bounds = [0]
    for ref in row_refs:
        bounds.append(bounds[-1] + ref.shape[0])
    for index, ref in enumerate(row_refs):
        labels_ref[:, bounds[index] : bounds[index + 1]] = ref[:, features:].T

    def products(panel):
        return [
            lax.dot_general(
                ref[:, :features],
                queries_ref[panel * STEP : (panel + 1) * STEP, :],
                (((1,), (1,)), ((), ())),
                preferred_element_type=jnp.float32,
            )
            for ref in row_refs
        ]

    rate = sharpness * math.log2(math.e)
    later = products(0)
    for panel in range(panels):
        now, later = later, products(panel + 1) if panel + 1 < panels else None
        columns = slice(panel * STEP, (panel + 1) * STEP)
        top = functools.reduce(jnp.maximum, [jnp.max(part, axis=0, keepdims=True) for part in now])
        if resumes:
            past_top = past_stats_ref[0:1, columns]
            top = jnp.maximum(top, past_top)
            fade = jnp.exp2((past_top - top) * rate)
        weights = [jnp.exp2((part - top) * rate).astype(jnp.bfloat16) for part in now]
        total = sum(
            jnp.sum(part.astype(jnp.float32), axis=0, keepdims=True) for part in weights
        )
        weighted = sum(
            jnp.dot(
                labels_ref[:, bounds[index] : bounds[index + 1]],
                part,
                preferred_element_type=jnp.float32,
            )
            for index, part in enumerate(weights)
        )
        if resumes:
            total = total + fade * past_stats_ref[1:2, columns]
            weighted = weighted + fade * past_ref[:, columns]
        if not ends:
            weighted_ref[:, columns] = weighted
            stats_ref[0:1, columns] = top
            stats_ref[1:2, columns] = total
            continue
        mean = (weighted * (1.0 / total)).astype(jnp.bfloat16)
        level = top * sharpness + jnp.log(total)
        first = level.astype(jnp.bfloat16).astype(jnp.float32)
        second = (level - first).astype(jnp.bfloat16).astype(jnp.float32)
        third = level - first - second
        row = lax.broadcasted_iota(jnp.int32, (EXTRA, STEP), 0)
        levels = jnp.where(
            row == 0, first, jnp.where(row == 1, second, jnp.where(row == 2, third, 0.0))
        ).astype(jnp.bfloat16)
        blocks, classes, wide = out_ref.shape
        classes -= EXTRA
        per_panel = blocks // panels
        for index in range(per_panel):
            block = panel * per_panel + index
            out_ref[block, :classes, :] = mean[:, index * wide : (index + 1) * wide]
            out_ref[block, classes:, :] = levels[:, index * wide : (index + 1) * wide]


def combine(parts_ref, out_ref):
    sources = parts_ref.shape[0]
    classes = parts_ref.shape[1] - EXTRA
    levels = [
        jnp.sum(parts_ref[source, classes:, :].astype(jnp.float32), axis=0, keepdims=True)
        for source in range(sources)
    ]
    top = functools.reduce(jnp.maximum, levels)
    shares = [jnp.exp(level - top) for level in levels]
    scale = 1.0 / sum(shares)
    shares = [share * scale for share in shares]
    for at in range(0, classes, 128):
        mean = sum(
            shares[source] * parts_ref[source, at : at + 128, :].astype(jnp.float32)
            for source in range(sources)
        )
        out_ref[:, at : at + 128] = mean.T.astype(out_ref.dtype)


def shards(queries, keys, labels):
    count, features = queries.shape
    classes = labels.shape[1]
    group = lax.axis_size(GROUP)
    inside = pl.BlockSpec(memory_space=pltpu.VMEM)
    sharpness = 2.5 / math.sqrt(features)

    panel = exchange(copies(queries, group), GROUP)

    rows = jnp.concatenate([keys, labels], axis=1)
    same = lax.all_gather(rows, "z_hi", axis=0, tiled=True)
    same, panel = lax.optimization_barrier((same, panel))
    others = [moved(same, -1, 0), moved(same, 0, 1), moved(same, 1, -1)]

    blocks = (group, classes + EXTRA, count)
    asked = group * count

    def taken(row_parts, running, ends):
        held = sum(part.shape[0] for part in row_parts)
        operands = [*row_parts, panel, *running]
        scratch = [pltpu.VMEM((classes, held), jnp.bfloat16)]
        if ends:
            out_specs = inside
            out_shape = jax.ShapeDtypeStruct(blocks, jnp.bfloat16)
        else:
            out_specs = [inside, inside]
            out_shape = [
                jax.ShapeDtypeStruct((classes, asked), jnp.float32),
                jax.ShapeDtypeStruct((8, asked), jnp.float32),
            ]
        return pl.pallas_call(
            functools.partial(classify, sharpness, len(row_parts), bool(running), ends),
            in_specs=[inside] * len(operands),
            out_specs=out_specs,
            out_shape=out_shape,
            scratch_shapes=scratch,
            compiler_params=pltpu.CompilerParams(vmem_limit_bytes=40 * 2**20),
            cost_estimate=pl.CostEstimate(
                flops=2 * asked * held * (features + classes),
                bytes_accessed=4 * 2**20,
                transcendentals=asked * held,
            ),
            name="classify",
        )(*operands)

    running = taken([same], (), False)
    same_late, running = lax.optimization_barrier((same, running))
    far_same = swapped(same_late)
    others, far_same = lax.optimization_barrier((others, far_same))
    others = jnp.concatenate(others, axis=0)
    running = taken([others, far_same], running, False)
    parts = taken([swapped(others)], running, True)
    parts = exchange(parts, GROUP)
    return pl.pallas_call(
        combine,
        out_shape=jax.ShapeDtypeStruct((count, classes), jnp.bfloat16),
        compiler_params=pltpu.CompilerParams(vmem_limit_bytes=20 * 2**20),
        cost_estimate=pl.CostEstimate(
            flops=2 * group * count * classes, bytes_accessed=3 * 2**20, transcendentals=0
        ),
        name="combine",
    )(parts)


def solution(mesh):
    chips = Mesh(mesh.devices.reshape(SIZES), AXES)
    placed = P(AXES, None)
    return jax.shard_map(
        shards, mesh=chips, in_specs=(placed, placed, placed), out_specs=placed, check_vma=False
    )
```
